256 devices in a mesh: row: 32 (over y, x, core), col: 8 (over z).
Axes of the slice: x: 4, y: 4, z: 8, core: 2. Of those that a mesh axis runs over, the one named last changes fastest.
Arguments:
- tokens: bfloat16 [512, 12288], P('row', 'col'), may hold values from -6 to 6
- weight_in: bfloat16 [12288, 24576], P('col', 'row'), may hold values from -0.0546875 to 0.0546875
- weight_out: bfloat16 [24576, 12288], P('row', 'col'), may hold values from -0.0390625 to 0.0390625
- cotangent: bfloat16 [512, 12288], P('row', 'col'), may hold values from -1.5 to 1.5
Outputs:
- output: bfloat16 [512, 12288], P('row', 'col')
- grad_tokens: bfloat16 [512, 12288], P('row', 'col')
- grad_weight_in: bfloat16 [12288, 24576], P('col', 'row')
- grad_weight_out: bfloat16 [24576, 12288], P('row', 'col')
The draws below stay inside these ranges and needn't reach their ends.
All inputs are finite; a program needn't handle non-finite values.
Results may differ from the reference program's by a relative error of at most 0.005.
Values may be sent and summed in bfloat16 or wider, within the bound.
A program may use at most 64 MiB of HBM per device.

```python
import jax
import jax.numpy as jnp
from jax import lax

D = 12288
FF = 24576
TOKENS = 512


def block_levels(rng, shape, split, least, high):
    def one(position, shards_of):
        draws = jax.random.uniform(jax.random.fold_in(jax.random.fold_in(rng, 6), position), (shards_of,), jnp.float32, least / len(split), high / len(split))
        return jnp.repeat(jnp.exp(draws), shape[position] // shards_of).reshape((-1,) + (1,) * (len(shape) - position - 1))

    gain = one(*split[0])
    for cut in split[1:]:
        gain = gain * one(*cut)
    return gain


def bell_draw(key, shape, scale, limit, shards=(), dtype=jnp.bfloat16):
    array = jax.random.normal(key, shape, jnp.float32) * scale
    if len(shards) > 0:
        array = block_levels(key, shape, shards, -0.22, 0.18) * array
    return jnp.clip(array, min=-limit, max=limit).astype(dtype)


def setup_inputs(seed: int = 0) -> dict:
    key_list = jax.random.split(jax.random.key(seed), 5)
    tokens = bell_draw(key_list[0], (TOKENS, D), 1.0, 6.0, ((0, 32), (1, 8)))
    weight_in = bell_draw(key_list[1], (D, FF), D ** -0.5, 0.0546875, ((0, 8), (1, 32)))
    weight_out = bell_draw(key_list[2], (FF, D), FF ** -0.5, 0.0390625, ((0, 32), (1, 8)))
    cotangent = bell_draw(key_list[3], (TOKENS, D), 0.25, 1.5, ((0, 32), (1, 8)))
    return {"tokens": tokens, "weight_in": weight_in, "weight_out": weight_out, "cotangent": cotangent}


gelu_scale = 0.7978845608028654
gelu_cubic = 0.044715


def activate(hidden):
    tangent = jnp.tanh(gelu_scale * (hidden + gelu_cubic * hidden * hidden * hidden))
    gelu_out = 0.5 * hidden * (1.0 + tangent)
    derivative = 0.5 * (1.0 + tangent) + 0.5 * hidden * (1.0 - tangent * tangent) * gelu_scale * (1.0 + 3.0 * gelu_cubic * hidden * hidden)
    return gelu_out, derivative


def contract_rows(left, right):
    return lax.dot_general(left, right, (((0,), (0,)), ((), ())), preferred_element_type=jnp.float32)


def contract_cols(left, right):
    return lax.dot_general(left, right, (((1,), (1,)), ((), ())), preferred_element_type=jnp.float32)


def reference(tokens, weight_in, weight_out, cotangent):
    hidden = jnp.dot(tokens, weight_in, preferred_element_type=jnp.float32)
    gelu_out, derivative = activate(hidden)
    activation = gelu_out.astype(jnp.bfloat16)
    output = jnp.dot(activation, weight_out, preferred_element_type=jnp.float32).astype(jnp.bfloat16)
    grad_activation = contract_cols(cotangent, weight_out)
    grad_hidden = (grad_activation * derivative).astype(jnp.bfloat16)
    grad_tokens = contract_cols(grad_hidden, weight_in).astype(jnp.bfloat16)
    grad_weight_in = contract_rows(tokens, grad_hidden).astype(jnp.bfloat16)
    grad_weight_out = contract_rows(activation, cotangent).astype(jnp.bfloat16)
    return (output, grad_tokens, grad_weight_in, grad_weight_out)
```

```python
import jax
import jax.numpy as jnp
from jax import lax
from jax.experimental import pallas as pl
from jax.experimental.pallas import tpu as pltpu
from jax.sharding import PartitionSpec as P

MESH = pl.DeviceIdType.MESH
F32, BF16 = jnp.float32, jnp.bfloat16
gelu_scale = 0.7978845608028654
gelu_cubic = 0.044715

NZ = 8
NX = NY = 4
ROWS = 16
TOK = 512
SHARD = TOK // NZ
HALF = SHARD // 2
FEAT = 1536
FH = FEAT // 2
HID = 768
NC = 3
W = HID // NC
N_SEM = 176


def activate(hidden):
    tangent = jnp.tanh(gelu_scale * (hidden + gelu_cubic * hidden * hidden * hidden))
    gelu_out = 0.5 * hidden * (1.0 + tangent)
    derivative = 0.5 * (1.0 + tangent) + 0.5 * hidden * (1.0 - tangent * tangent) * gelu_scale * (
        1.0 + 3.0 * gelu_cubic * hidden * hidden
    )
    return (gelu_out, derivative)


def mm(left, right):
    return lax.dot_general(left, right, (((1,), (0,)), ((), ())), preferred_element_type=F32)


def mm_nt(left, right):
    return lax.dot_general(left, right, (((1,), (1,)), ((), ())), preferred_element_type=F32)


def mm_tn(left, right):
    return lax.dot_general(left, right, (((0,), (0,)), ((), ())), preferred_element_type=F32)


def kernel(
    tok_hbm, wi_hbm, wo_hbm, cot_hbm,
    out_ref, gt_ref, gwi_hbm, gwo_hbm,
    wi, wo, tok, cot, hid, gac, zsnd, zrcv, act, grd, slope,
    psnd, prcv, own, lsnd, lrcv, ssnd, srcv, gwi, gwo,
    ssem, rsem, lsem,
):
    row, z = lax.axis_index("row"), lax.axis_index("col")
    c, x, y = lax.rem(row, 2), lax.rem(row // 2, NX), row // (2 * NX)

    def at(dc, dy, dx, dz):
        yy, xx = lax.rem(y + dy, NY), lax.rem(x + dx, NX)
        cc = 1 - c if dc else c
        return ((yy * NX + xx) * 2 + cc, lax.rem(z + dz, NZ))

    def along(axis, d):
        return at(0, d, 0, 0) if axis == "y" else at(0, 0, d, 0)

    sibling, z_up, z_down = at(1, 0, 0, 0), at(0, 0, 0, 1), at(0, 0, 0, NZ - 1)

    used = [0]
    sends = []

    def send(src, dst, dev):
        i = used[0]
        used[0] += 1
        copy = pltpu.make_async_remote_copy(
            src_ref=src, dst_ref=dst, send_sem=ssem.at[i], recv_sem=rsem.at[i],
            device_id=dev, device_id_type=MESH,
        )
        copy.start()
        sends.append(copy)
        return copy

    local = []

    def fetch(src, dst):
        copy = pltpu.make_async_copy(src, dst, lsem.at[len(local)])
        copy.start()
        local.append(copy)
        return copy

    got_tok = [fetch(tok_hbm.at[:, pl.ds(h * FH, FH)], tok.at[h, 0, 0, 0]) for h in (0, 1)]
    got_cot = [fetch(cot_hbm.at[:, pl.ds(h * FH, FH)], cot.at[h, 0, 0, 0]) for h in (0, 1)]
    got_wi = fetch(wi_hbm, wi)
    got_wo = fetch(wo_hbm, wo)

    barrier = pltpu.get_barrier_semaphore()
    partners = [sibling, z_up, z_down] + [along(a, d) for a in ("x", "y") for d in (1, 2, 3)]
    for dev in partners:
        pl.semaphore_signal(barrier, inc=1, device_id=dev, device_id_type=MESH)
    pl.semaphore_wait(barrier, len(partners))

    first, second = ("x", "y"), ("y", "x")

    def slots(ref, h, dc, da, db):
        sl = [slice(None) if d is None else d for d in (da, db)]
        dy, dx = (sl[1], sl[0]) if first[h] == "x" else (sl[0], sl[1])
        return ref.at[h, dc, dy, dx]

    def gather_first(ref, got):
        a, b = {}, {}
        for h in (0, 1):
            got[h].wait()
            for d in (1, 3, 2):
                a[h, d] = send(slots(ref, h, 0, 0, 0), slots(ref, h, 0, 4 - d, 0), along(first[h], d))
            for d in (1, 3, 2):
                b[h, d] = send(slots(ref, h, 0, 0, 0), slots(ref, h, 0, 0, 4 - d), along(second[h], d))
        return a, b

    def gather_second(ref, a):
        g = {}
        for h in (0, 1):
            for d in (1, 3, 2):
                a[h, d].wait_recv()
            for d in (1, 3, 2):
                dev = along(second[h], d)
                g[h, d] = send(slots3(ref, h, 0), slots3(ref, h, 4 - d), dev)
        return g

    def slots3(ref, h, db):
        if first[h] == "x":
            return ref.at[h, 0, db, pl.ds(1, 3)]
        return ref.at[h, 0, pl.ds(1, 3), db]

    def gather_near(ref):
        return {(h, 0): send(slots(ref, h, 0, None, 0), slots(ref, h, 1, None, 0), sibling) for h in (0, 1)}

    def gather_far(ref, b, g):
        s = {}
        for d in (1, 3, 2):
            for h in (0, 1):
                b[h, d].wait_recv()
                g[h, d].wait_recv()
                e = 4 - d
                s[h, e] = send(slots(ref, h, 0, None, e), slots(ref, h, 1, None, e), sibling)
        return s

    def rows(ref, h):
        return ref[h].reshape(TOK, FH)

    def reduce_step(n, part, j, t, got):
        for way, dev in ((0, z_up), (1, z_down)):
            share = lax.rem(z + (5 - t if way == 0 else 3 + t), NZ)
            near = pl.ds(way * HALF, HALF)
            buf = zsnd.at[n, j, way, t - 1]
            if t == 1:
                buf[near] = part[j, share, near].astype(BF16)
                src, dst = buf.at[near], zrcv.at[n, j, way, t - 1, near]
            else:
                got[way, t - 1].wait_recv()
                if t == 2:
                    far = pl.ds((1 - way) * HALF, HALF)
                    buf[near] = (part[j, share, near] + zrcv[n, j, way, 0, near].astype(F32)).astype(BF16)
                    buf[far] = part[j, share, far].astype(BF16)
                else:
                    buf[...] = (part[j, share] + zrcv[n, j, way, t - 2].astype(F32)).astype(BF16)
                src, dst = buf, zrcv.at[n, j, way, t - 1]
            got[way, t] = send(src, dst, dev)

    def reduce_end(n, part, j, got):
        got[0, 4].wait_recv()
        got[1, 4].wait_recv()
        return part[j, z] + zrcv[n, j, 0, 3].astype(F32) + zrcv[n, j, 1, 3].astype(F32)

    def spread_step(ref, j, t, got):
        for way, dev in ((0, z_up), (1, z_down)):
            share = lax.rem(z + (NZ + 1 - t if way == 0 else t - 1), NZ)
            if t > 1:
                got[way, t - 1].wait_recv()
            block = ref.at[j, share]
            if t == 4:
                block = block.at[pl.ds(way * HALF, HALF)]
            got[way, t] = send(block, block, dev)

    def spread_end(got):
        got[0, 4].wait_recv()
        got[1, 4].wait_recv()

    def scatter_pair(n, h, value):
        own[n, h] = value[: TOK // 2].reshape(NY, NX, ROWS, FH)
        psnd[n, h] = value[TOK // 2 :].reshape(NY, NX, ROWS, FH)
        return send(psnd.at[n, h], prcv.at[n, h], sibling)

    def scatter_first(n, h, got):
        got.wait_recv()
        res = {}
        for d in (2, 1, 3):
            if first[h] == "x":
                val = own[n, h, d] + prcv[n, h, d]
            else:
                val = own[n, h, :, d] + prcv[n, h, :, d]
            lsnd[n, h, d - 1] = val.astype(BF16)
            res[d] = send(lsnd.at[n, h, d - 1], lrcv.at[n, h, d - 1], along(second[h], d))
        if first[h] == "x":
            own[n, h, 0] = own[n, h, 0] + prcv[n, h, 0]
        else:
            own[n, h, :, 0] = own[n, h, :, 0] + prcv[n, h, :, 0]
        return res

    def scatter_second(n, h, got):
        for d in (1, 3, 2):
            got[d].wait_recv()
        res = {}
        base = own[n, h, 0] if first[h] == "x" else own[n, h, :, 0]
        total = base + lrcv[n, h, 0].astype(F32) + lrcv[n, h, 1].astype(F32) + lrcv[n, h, 2].astype(F32)
        ssnd[n, h] = total
        for d in (2, 1, 3):
            res[d] = send(ssnd.at[n, h, d], srcv.at[n, h, d - 1], along(first[h], d))
        return res

    def scatter_end(n, h, got, ref):
        for d in (1, 3, 2):
            got[d].wait_recv()
        total = ssnd[n, h, 0] + srcv[n, h, 0] + srcv[n, h, 1] + srcv[n, h, 2]
        ref[:, pl.ds(h * FH, FH)] = total.astype(BF16)

    chunks = range(NC)

    a, b = gather_first(tok, got_tok)
    ca, cb = gather_first(cot, got_cot)
    g = gather_second(tok, a)
    near = gather_near(tok)
    far = gather_far(tok, b, g)
    cg = gather_second(cot, ca)
    cnear = gather_near(cot)
    got_wi.wait()
    for s in (near, far):
        for copy in s.values():
            copy.wait_recv()

    hg = [{} for _ in chunks]
    gg = [{} for _ in chunks]
    for j in chunks:
        cols = pl.ds(j * W, W)
        value = mm(rows(tok, 0), wi[pl.ds(0, FH), cols]) + mm(rows(tok, 1), wi[pl.ds(FH, FH), cols])
        hid[j] = value.reshape(NZ, SHARD, W)
        reduce_step(0, hid, j, 1, hg[j])
    cfar = gather_far(cot, cb, cg)
    for j in chunks:
        reduce_step(0, hid, j, 2, hg[j])
    got_wo.wait()
    for s in (cnear, cfar):
        for copy in s.values():
            copy.wait_recv()
    for j in chunks:
        cols = pl.ds(j * W, W)
        value = mm_nt(rows(cot, 0), wo[cols, pl.ds(0, FH)]) + mm_nt(rows(cot, 1), wo[cols, pl.ds(FH, FH)])
        gac[j] = value.reshape(NZ, SHARD, W)
        reduce_step(1, gac, j, 1, gg[j])
    for t in (3, 4):
        for j in chunks:
            reduce_step(0, hid, j, t, hg[j])
        for j in chunks:
            reduce_step(1, gac, j, t - 1, gg[j])
    ag = [{} for _ in chunks]
    bg = [{} for _ in chunks]
    for j in chunks:
        gelu_out, derivative = activate(reduce_end(0, hid, j, hg[j]))
        act[j, z] = gelu_out.astype(BF16)
        slope[j] = derivative
        spread_step(act, j, 1, ag[j])
    for j in chunks:
        reduce_step(1, gac, j, 4, gg[j])
    for j in chunks:
        spread_step(act, j, 2, ag[j])
    for j in chunks:
        grd[j, z] = (reduce_end(1, gac, j, gg[j]) * slope[j]).astype(BF16)
        spread_step(grd, j, 1, bg[j])
    for t in (3, 4):
        for j in chunks:
            spread_step(act, j, t, ag[j])
        for j in chunks:
            spread_step(grd, j, t - 1, bg[j])
    for j in chunks:
        spread_end(ag[j])

    op = []
    for h in (0, 1):
        value = jnp.zeros((TOK, FH), F32)
        for j in chunks:
            value = value + mm(act[j].reshape(TOK, W), wo[pl.ds(j * W, W), pl.ds(h * FH, FH)])
        op.append(scatter_pair(0, h, value))
    for j in chunks:
        spread_step(grd, j, 4, bg[j])
    for j in chunks:
        spread_end(bg[j])
    gp = []
    for h in (0, 1):
        value = jnp.zeros((TOK, FH), F32)
        for j in chunks:
            value = value + mm_nt(grd[j].reshape(TOK, W), wi[pl.ds(h * FH, FH), pl.ds(j * W, W)])
        gp.append(scatter_pair(1, h, value))
        if h == 0:
            o1 = [scatter_first(0, k, op[k]) for k in (0, 1)]
    for j in chunks:
        for h in (0, 1):
            gwo[pl.ds(j * W, W), pl.ds(h * FH, FH)] = mm_tn(act[j].reshape(TOK, W), rows(cot, h)).astype(BF16)
    put_gwo = fetch(gwo, gwo_hbm)
    g1 = [scatter_first(1, h, gp[h]) for h in (0, 1)]
    o2 = [scatter_second(0, h, o1[h]) for h in (0, 1)]
    for h in (0, 1):
        for j in chunks:
            gwi[pl.ds(h * FH, FH), pl.ds(j * W, W)] = mm_tn(rows(tok, h), grd[j].reshape(TOK, W)).astype(BF16)
    put_gwi = fetch(gwi, gwi_hbm)
    g2 = [scatter_second(1, h, g1[h]) for h in (0, 1)]
    for h in (0, 1):
        scatter_end(0, h, o2[h], out_ref)
    for h in (0, 1):
        scatter_end(1, h, g2[h], gt_ref)
    put_gwo.wait()
    put_gwi.wait()
    for copy in sends:
        copy.wait_send()
    assert used[0] <= N_SEM, used[0]


def per_device(tokens, weight_in, weight_out, cotangent):
    any_spec = pl.BlockSpec(memory_space=pl.ANY)
    vmem = pl.BlockSpec(memory_space=pltpu.VMEM)
    shape = jax.ShapeDtypeStruct
    return pl.pallas_call(
        kernel,
        out_shape=(
            shape((ROWS, FEAT), BF16), shape((ROWS, FEAT), BF16), shape((FEAT, HID), BF16), shape((HID, FEAT), BF16),
        ),
        in_specs=[any_spec] * 4,
        out_specs=(vmem, vmem, any_spec, any_spec),
        scratch_shapes=[
            pltpu.VMEM((FEAT, HID), BF16),
            pltpu.VMEM((HID, FEAT), BF16),
            pltpu.VMEM((2, 2, NY, NX, ROWS, FH), BF16),
            pltpu.VMEM((2, 2, NY, NX, ROWS, FH), BF16),
            pltpu.VMEM((NC, NZ, SHARD, W), F32),
            pltpu.VMEM((NC, NZ, SHARD, W), F32),
            pltpu.VMEM((2, NC, 2, 4, SHARD, W), BF16),
            pltpu.VMEM((2, NC, 2, 4, SHARD, W), BF16),
            pltpu.VMEM((NC, NZ, SHARD, W), BF16),
            pltpu.VMEM((NC, NZ, SHARD, W), BF16),
            pltpu.VMEM((NC, SHARD, W), F32),
            pltpu.VMEM((2, 2, NY, NX, ROWS, FH), F32),
            pltpu.VMEM((2, 2, NY, NX, ROWS, FH), F32),
            pltpu.VMEM((2, 2, NY, NX, ROWS, FH), F32),
            pltpu.VMEM((2, 2, 3, 4, ROWS, FH), BF16),
            pltpu.VMEM((2, 2, 3, 4, ROWS, FH), BF16),
            pltpu.VMEM((2, 2, 4, ROWS, FH), F32),
            pltpu.VMEM((2, 2, 3, ROWS, FH), F32),
            pltpu.VMEM((FEAT, HID), BF16),
            pltpu.VMEM((HID, FEAT), BF16),
            pltpu.SemaphoreType.DMA((N_SEM,)),
            pltpu.SemaphoreType.DMA((N_SEM,)),
            pltpu.SemaphoreType.DMA((8,)),
        ],
        compiler_params=pltpu.CompilerParams(
            collective_id=0, has_side_effects=True, vmem_limit_bytes=52 * 2**20
        ),
        cost_estimate=pl.CostEstimate(flops=7 * 10**9, bytes_accessed=10**7, transcendentals=5 * 10**4),
    )(tokens, weight_in, weight_out, cotangent)


def solution(mesh):
    in_specs = (P("row", "col"), P("col", "row"), P("row", "col"), P("row", "col"))
    out_specs = (P("row", "col"), P("row", "col"), P("col", "row"), P("row", "col"))
    return jax.shard_map(
        per_device, mesh=mesh, in_specs=in_specs, out_specs=out_specs, check_vma=False
    )
```

```python
import jax
import jax.numpy as jnp
from jax import lax
from jax.experimental import pallas as pl
from jax.experimental.pallas import tpu as pltpu
from jax.sharding import PartitionSpec as P

MESH = pl.DeviceIdType.MESH
F32, BF16 = jnp.float32, jnp.bfloat16
gelu_scale = 0.7978845608028654
gelu_cubic = 0.044715

NZ = 8
NX = NY = 4
ROWS = 16
MINE = NY * NX * ROWS
SHARD = MINE // NZ
HALF = SHARD // 2
LINE = NX * ROWS
FEAT = 1536
FH = FEAT // 2
HID = 768


def activate(hidden):
    tangent = jnp.tanh(gelu_scale * (hidden + gelu_cubic * hidden * hidden * hidden))
    gelu_out = 0.5 * hidden * (1.0 + tangent)
    derivative = 0.5 * (1.0 + tangent) + 0.5 * hidden * (1.0 - tangent * tangent) * gelu_scale * (
        1.0 + 3.0 * gelu_cubic * hidden * hidden
    )
    return (gelu_out, derivative)


def mm(left, right):
    return lax.dot_general(left, right, (((1,), (0,)), ((), ())), preferred_element_type=F32)


def mm_nt(left, right):
    return lax.dot_general(left, right, (((1,), (1,)), ((), ())), preferred_element_type=F32)


def mm_tn(left, right):
    return lax.dot_general(left, right, (((0,), (0,)), ((), ())), preferred_element_type=F32)


def kernel(
    tok_hbm, wi_hbm, wo_hbm, cot_hbm,
    out_ref, gt_ref, gwi, gwo,
    wi, wo, wi2, wo2, tok, cot, part, zsnd, zrcv, act, grd, slope, own, lsnd, lrcv, ssnd, srcv,
    ssem, rsem, lsem,
):
    row, z = lax.axis_index("row"), lax.axis_index("col")
    c, x, y = lax.rem(row, 2), lax.rem(row // 2, NX), row // (2 * NX)

    def at(cc, dy, dx, dz):
        return ((lax.rem(y + dy, NY) * NX + lax.rem(x + dx, NX)) * 2 + cc, lax.rem(z + dz, NZ))

    def along(axis, d):
        return at(c, d, 0, 0) if axis == "y" else at(c, 0, d, 0)

    sibling, z_up, z_down = at(1 - c, 0, 0, 0), at(c, 0, 0, 1), at(c, 0, 0, NZ - 1)

    names = {}

    def sem(pool, name):
        known = names.setdefault(id(pool), {})
        return pool.at[known.setdefault(name, len(known))]

    def copy_to(src, dst, s, r, dev):
        return pltpu.make_async_remote_copy(
            src_ref=src, dst_ref=dst, send_sem=sem(ssem, s), recv_sem=sem(rsem, r),
            device_id=dev, device_id_type=MESH,
        )

    sent = {}

    def send(src, dst, s, r, dev):
        copy_to(src, dst, s, r, dev).start()
        size = 1
        for n in src.shape:
            size *= n
        sent[s] = sent.get(s, 0) + size * src.dtype.itemsize

    def arrived(like, r):
        copy_to(like, like, "none", r, sibling).wait_recv()

    def all_sent(s):
        n = sent[s] // (HID * 2)
        assert n * HID * 2 == sent[s] and n <= FEAT, (s, n)
        copy_to(wi.at[pl.ds(0, n)], wi.at[pl.ds(0, n)], s, "none", sibling).wait_send()

    def fetch(src, dst, name):
        copy = pltpu.make_async_copy(src, dst, sem(lsem, name))
        copy.start()
        return copy

    got_tok = fetch(tok_hbm, tok.at[pl.ds(0, ROWS)], "tok")
    got_cot = fetch(cot_hbm, cot.at[pl.ds(0, ROWS)], "cot")
    got_wi = fetch(wi_hbm, wi, "wi")
    got_wo = fetch(wo_hbm, wo, "wo")

    barrier = pltpu.get_barrier_semaphore()
    partners = [sibling, z_up, z_down] + [along(a, d) for a in ("x", "y") for d in (1, 2, 3)]
    for dev in partners:
        pl.semaphore_signal(barrier, inc=1, device_id=dev, device_id_type=MESH)
    pl.semaphore_wait(barrier, len(partners))

    first, second = ("x", "y"), ("y", "x")

    def block(ref, h, da, db):
        dy, dx = (db, da) if first[h] == "x" else (da, db)
        return ref.at[pl.ds((dy * NX + dx) * ROWS, ROWS), pl.ds(h * FH, FH)]

    def gather_first(ref, name):
        for h in (0, 1):
            for d in (1, 3, 2):
                send(block(ref, h, 0, 0), block(ref, h, 4 - d, 0), "gather", (name, "a", h), along(first[h], d))
        for h in (0, 1):
            for d in (1, 3, 2):
                send(block(ref, h, 0, 0), block(ref, h, 0, 4 - d), "gather", (name, "b"), along(second[h], d))

    def gather_second(ref, name):
        for h in (0, 1):
            arrived(ref.at[pl.ds(ROWS, 3 * ROWS), pl.ds(h * FH, FH)], (name, "a", h))
            for d in (1, 3, 2):
                if first[h] == "x":
                    cols = pl.ds(h * FH, FH)
                    send(
                        ref.at[pl.ds(ROWS, 3 * ROWS), cols], ref.at[pl.ds((4 - d) * LINE + ROWS, 3 * ROWS), cols],
                        "gather", (name, "b"), along(second[h], d),
                    )
                else:
                    for e in (1, 2, 3):
                        send(block(ref, h, e, 0), block(ref, h, e, 4 - d), "gather", (name, "b"), along(second[h], d))

    def gather_end(ref, name):
        arrived(ref.at[pl.ds(LINE, 3 * LINE)], (name, "b"))

    def share_rows(dz):
        return pl.ds(pl.multiple_of(lax.rem(z + dz, NZ) * SHARD, SHARD), SHARD)

    def half_rows(dz, way):
        return pl.ds(pl.multiple_of(lax.rem(z + dz, NZ) * SHARD + way * HALF, HALF), HALF)

    def reduce_step(n, k, t):
        if t > 1:
            arrived(zrcv.at[n, k, t - 2, 0] if t == 2 else zrcv.at[n, k, t - 2], ("r", n, k, t - 1))
        for way, dev in ((0, z_up), (1, z_down)):
            dz = 5 - t if way == 0 else 3 + t
            near, far = pl.ds(way * HALF, HALF), pl.ds((1 - way) * HALF, HALF)
            buf, dst = zsnd.at[n, k, t - 1, way], zrcv.at[n, k, t - 1, way]
            if t == 1:
                buf[near] = part[n, k, half_rows(dz, way)].astype(BF16)
                buf, dst = buf.at[near], dst.at[near]
            elif t == 2:
                buf[near] = (part[n, k, half_rows(dz, way)] + zrcv[n, k, 0, way, near].astype(F32)).astype(BF16)
                buf[far] = part[n, k, half_rows(dz, 1 - way)].astype(BF16)
            else:
                buf[...] = (part[n, k, share_rows(dz)] + zrcv[n, k, t - 2, way].astype(F32)).astype(BF16)
            send(buf, dst, ("z", n), ("r", n, k, t), dev)

    def reduce_end(n, k):
        arrived(zrcv.at[n, k, 3], ("r", n, k, 4))
        return part[n, k, share_rows(0)] + zrcv[n, k, 3, 0].astype(F32) + zrcv[n, k, 3, 1].astype(F32)

    def spread_step(n, ref, k, t):
        if t > 1:
            arrived(zrcv.at[n, k, 3], ("s", n, k, t - 1))
        for way, dev in ((0, z_up), (1, z_down)):
            dz = NZ + 1 - t if way == 0 else t - 1
            piece = ref.at[2 * k, half_rows(dz, way) if t == 4 else share_rows(dz)]
            send(piece, piece, ("z", n), ("s", n, k, t), dev)

    def spread_end(n, k):
        arrived(zrcv.at[n, k, 3, 0], ("s", n, k, 4))

    def scatter_first(n, h, value):
        for d in (2, 1, 3, 0):
            if first[h] == "x":
                val = value[d * LINE : (d + 1) * LINE]
            else:
                val = jnp.concatenate([value[e * LINE + d * ROWS : e * LINE + (d + 1) * ROWS] for e in range(NY)], axis=0)
            if d == 0:
                own[n, h] = val
            else:
                lsnd[n, h, d - 1] = val.astype(BF16)
                send(lsnd.at[n, h, d - 1], lrcv.at[n, h, d - 1], ("l", n), ("l", n, h), along(second[h], d))

    def scatter_second(n, h):
        arrived(lrcv.at[n, h], ("l", n, h))
        ssnd[n, h] = own[n, h] + lrcv[n, h, 0].astype(F32) + lrcv[n, h, 1].astype(F32) + lrcv[n, h, 2].astype(F32)
        for d in (2, 1, 3):
            rows = pl.ds(d * ROWS, ROWS)
            send(ssnd.at[n, h, rows], srcv.at[n, h, d - 1], ("l", n), ("m", n, h), along(first[h], d))

    def scatter_end(n, h, ref):
        arrived(srcv.at[n, h], ("m", n, h))
        total = ssnd[n, h, pl.ds(0, ROWS)] + srcv[n, h, 0] + srcv[n, h, 1] + srcv[n, h, 2]
        ref[:, pl.ds(h * FH, FH)] = total.astype(BF16)

    mine, theirs = pl.ds(0, MINE), pl.ds(MINE, MINE)
    halves = (0, 1)

    got_tok.wait()
    gather_first(tok, "tok")
    got_wi.wait()
    send(wi, wi2, "wi", "wi", sibling)
    got_cot.wait()
    gather_first(cot, "cot")
    got_wo.wait()
    send(wo, wo2, "wo", "wo", sibling)
    gather_second(tok, "tok")
    gather_end(tok, "tok")
    gather_second(cot, "cot")

    part[0, 0] = mm(tok[mine], wi[...])
    reduce_step(0, 0, 1)
    arrived(wi2, "wi")
    part[0, 1] = mm(tok[mine], wi2[...])
    reduce_step(0, 1, 1)
    reduce_step(0, 0, 2)
    reduce_step(0, 1, 2)
    gather_end(cot, "cot")
    part[1, 0] = mm_nt(cot[mine], wo[...])
    reduce_step(1, 0, 1)
    arrived(wo2, "wo")
    part[1, 1] = mm_nt(cot[mine], wo2[...])
    reduce_step(1, 1, 1)
    send(tok.at[mine], tok.at[theirs], "near", "tok2", sibling)
    send(cot.at[mine], cot.at[theirs], "near", "cot2", sibling)
    for t in (3, 4):
        for k in halves:
            reduce_step(0, k, t)
        for k in halves:
            reduce_step(1, k, t - 1)
    for k in halves:
        gelu_out, derivative = activate(reduce_end(0, k))
        act[2 * k, share_rows(0)] = gelu_out.astype(BF16)
        slope[k] = derivative
        spread_step(0, act, k, 1)
    for k in halves:
        reduce_step(1, k, 4)
    for k in halves:
        spread_step(0, act, k, 2)
    for k in halves:
        grd[2 * k, share_rows(0)] = (reduce_end(1, k) * slope[k]).astype(BF16)
        spread_step(1, grd, k, 1)
    for t in (3, 4):
        for k in halves:
            spread_step(0, act, k, t)
        for k in halves:
            spread_step(1, grd, k, t - 1)
    for k in halves:
        spread_end(0, k)
    send(act.at[2], act.at[1], "near", "act2", sibling)
    for h in halves:
        cols = pl.ds(h * FH, FH)
        scatter_first(0, h, mm(act[0], wo[:, cols]) + mm(act[2], wo2[:, cols]))
        spread_step(1, grd, h, 4)
    arrived(tok.at[theirs], "tok2")
    arrived(cot.at[theirs], "cot2")
    arrived(act.at[1], "act2")
    gwo[...] = mm_tn(act[pl.ds(0, 2)].reshape(2 * MINE, HID), cot[...]).astype(BF16)
    for k in halves:
        spread_end(1, k)
    send(grd.at[2], grd.at[1], "near", "grd2", sibling)
    for h in halves:
        cols = pl.ds(h * FH, FH)
        scatter_first(1, h, mm_nt(grd[0], wi[cols, :]) + mm_nt(grd[2], wi2[cols, :]))
    for h in halves:
        scatter_second(0, h)
    arrived(grd.at[1], "grd2")
    gwi[...] = mm_tn(tok[...], grd[pl.ds(0, 2)].reshape(2 * MINE, HID)).astype(BF16)
    for h in halves:
        scatter_second(1, h)
    for h in halves:
        scatter_end(0, h, out_ref)
    for h in halves:
        scatter_end(1, h, gt_ref)
    for s in sent:
        all_sent(s)
    for pool, known in ((ssem, 12), (rsem, 64), (lsem, 4)):
        assert len(names[id(pool)]) <= known


def hand_over(*refs):
    srcs, dsts, sems = refs[:4], refs[4:8], refs[8]
    copies = []
    for s, d in zip(srcs, dsts):
        parts = s.shape[0] // 192 or 1
        for p in range(parts):
            rows = pl.ds(p * (s.shape[0] // parts), s.shape[0] // parts)
            copies.append(pltpu.make_async_copy(s.at[rows], d.at[rows], sems.at[len(copies)]))
    for copy in copies:
        copy.start()
    for copy in copies:
        copy.wait()


def per_device(tokens, weight_in, weight_out, cotangent):
    hbm = pl.BlockSpec(memory_space=pltpu.HBM)
    vmem = pl.BlockSpec(memory_space=pltpu.VMEM)
    shape = jax.ShapeDtypeStruct
    shapes = (
        shape((ROWS, FEAT), BF16), shape((ROWS, FEAT), BF16), shape((FEAT, HID), BF16), shape((HID, FEAT), BF16),
    )
    tokens, cotangent = [pltpu.with_memory_space_constraint(a, pltpu.HBM) for a in (tokens, cotangent)]
    results = pl.pallas_call(
        kernel,
        out_shape=shapes,
        in_specs=[hbm] * 4,
        out_specs=(vmem,) * 4,
        scratch_shapes=[
            pltpu.VMEM((FEAT, HID), BF16),
            pltpu.VMEM((HID, FEAT), BF16),
            pltpu.VMEM((FEAT, HID), BF16),
            pltpu.VMEM((HID, FEAT), BF16),
            pltpu.VMEM((2 * MINE, FEAT), BF16),
            pltpu.VMEM((2 * MINE, FEAT), BF16),
            pltpu.VMEM((2, 2, MINE, HID), F32),
            pltpu.VMEM((2, 2, 4, 2, SHARD, HID), BF16),
            pltpu.VMEM((2, 2, 4, 2, SHARD, HID), BF16),
            pltpu.VMEM((3, MINE, HID), BF16),
            pltpu.VMEM((3, MINE, HID), BF16),
            pltpu.VMEM((2, SHARD, HID), F32),
            pltpu.VMEM((2, 2, LINE, FH), F32),
            pltpu.VMEM((2, 2, 3, LINE, FH), BF16),
            pltpu.VMEM((2, 2, 3, LINE, FH), BF16),
            pltpu.VMEM((2, 2, LINE, FH), F32),
            pltpu.VMEM((2, 2, 3, ROWS, FH), F32),
            pltpu.SemaphoreType.DMA((12,)),
            pltpu.SemaphoreType.DMA((64,)),
            pltpu.SemaphoreType.DMA((4,)),
        ],
        compiler_params=pltpu.CompilerParams(
            collective_id=0, has_side_effects=True, vmem_limit_bytes=48 * 2**20
        ),
        cost_estimate=pl.CostEstimate(flops=7 * 10**9, bytes_accessed=10**7, transcendentals=5 * 10**4),
    )(tokens, weight_in, weight_out, cotangent)
    return pl.pallas_call(
        hand_over,
        out_shape=shapes,
        in_specs=[vmem] * 4,
        out_specs=(hbm,) * 4,
        scratch_shapes=[pltpu.SemaphoreType.DMA((14,))],
        compiler_params=pltpu.CompilerParams(vmem_limit_bytes=2**21),
        cost_estimate=pl.CostEstimate(flops=0, bytes_accessed=10**7, transcendentals=0),
    )(*results)


def solution(mesh):
    in_specs = (P("row", "col"), P("col", "row"), P("row", "col"), P("row", "col"))
    out_specs = (P("row", "col"), P("row", "col"), P("col", "row"), P("row", "col"))
    return jax.shard_map(
        per_device, mesh=mesh, in_specs=in_specs, out_specs=out_specs, check_vma=False
    )
```

```python
import jax
import jax.numpy as jnp
from jax import lax
from jax.experimental import pallas as pl
from jax.experimental.pallas import tpu as pltpu
from jax.sharding import PartitionSpec as P

MESH = pl.DeviceIdType.MESH
F32, BF16 = jnp.float32, jnp.bfloat16
gelu_scale = 0.7978845608028654
gelu_cubic = 0.044715

NZ = 8
NX = NY = 4
ROWS = 16
MINE = NY * NX * ROWS
CHUNK = MINE // 2
PAIR = 2 * ROWS
FEAT = 1536
FH = FEAT // 2
HID = 768
N_SEND, N_RECV = 12, 72


def activate(hidden):
    tangent = jnp.tanh(gelu_scale * (hidden + gelu_cubic * hidden * hidden * hidden))
    gelu_out = 0.5 * hidden * (1.0 + tangent)
    derivative = 0.5 * (1.0 + tangent) + 0.5 * hidden * (1.0 - tangent * tangent) * gelu_scale * (
        1.0 + 3.0 * gelu_cubic * hidden * hidden
    )
    return (gelu_out, derivative)


def mm(left, right):
    return lax.dot_general(left, right, (((1,), (0,)), ((), ())), preferred_element_type=F32)


def mm_tn(left, right):
    return lax.dot_general(left, right, (((0,), (0,)), ((), ())), preferred_element_type=F32)


def kernel(
    tok_hbm, wi_hbm, wo_hbm, cot_hbm,
    out_ref, gt_ref, gwi, gwo,
    wi, wo, wit, wot, tok, cot, part, zsnd, zrcv, act, grd, act2, grd2, slope, tmp, own, lsnd, lrcv, ssnd, srcv,
    ssem, rsem, lsem,
):
    row, z = lax.axis_index("row"), lax.axis_index("col")
    c, x, y = lax.rem(row, 2), lax.rem(row // 2, NX), row // (2 * NX)
    parity = lax.rem(x + y, 2)
    stages = halves = (0, 1)
    chunk = [lax.rem(r + parity, 2) for r in stages]

    def at(cc, dy, dx, dz):
        return ((lax.rem(y + dy, NY) * NX + lax.rem(x + dx, NX)) * 2 + cc, lax.rem(z + dz, NZ))

    def along(axis, d):
        return at(c, d, 0, 0) if axis == "y" else at(c, 0, d, 0)

    sibling, z_up, z_down = at(1 - c, 0, 0, 0), at(c, 0, 0, 1), at(c, 0, 0, NZ - 1)

    names = {}

    def sem(pool, name):
        known = names.setdefault(id(pool), {})
        return pool.at[known.setdefault(name, len(known))]

    def copy_to(src, dst, s, r, dev):
        return pltpu.make_async_remote_copy(
            src_ref=src, dst_ref=dst, send_sem=sem(ssem, s), recv_sem=sem(rsem, r),
            device_id=dev, device_id_type=MESH,
        )

    sent = {}

    def send(src, dst, s, r, dev, counts=True):
        copy_to(src, dst, s, r, dev).start()
        size = src.dtype.itemsize if counts else 0
        for n in src.shape:
            size *= n
        sent[s] = sent.get(s, 0) + size

    def arrived(like, r):
        copy_to(like, like, "none", r, sibling).wait_recv()

    def all_sent(s):
        n = sent[s] // (HID * 2)
        assert n * HID * 2 == sent[s] and n <= FEAT, (s, n)
        like = wi.at[pl.ds(0, n), pl.ds(0, HID)]
        copy_to(like, like, s, "none", sibling).wait_send()

    def fetch(src, dst, name):
        copy = pltpu.make_async_copy(src, dst, sem(lsem, name))
        copy.start()
        return copy

    def rows16(i):
        return pl.ds(i * ROWS if isinstance(i, int) else pl.multiple_of(i * ROWS, ROWS), ROWS)

    mine, theirs = pl.ds(0, HID), pl.ds(HID, HID)

    got_tok = fetch(tok_hbm, tok.at[0, rows16(0)], "tok")
    got_cot = fetch(cot_hbm, cot.at[0, rows16(0)], "cot")
    got_wi = fetch(wi_hbm, wi.at[:, mine], "wi")
    got_wo = fetch(wo_hbm, wo.at[mine], "wo")

    barrier = pltpu.get_barrier_semaphore()
    partners = [sibling, z_up, z_down] + [along(a, d) for a in ("x", "y") for d in (1, 2, 3)]
    for dev in partners:
        pl.semaphore_signal(barrier, inc=1, device_id=dev, device_id_type=MESH)
    pl.semaphore_wait(barrier, len(partners))

    first, second = ("x", "y"), ("y", "x")
    cols = [pl.ds(h * FH, FH) for h in halves]

    def gather_first(ref, name):
        for h in halves:
            for d in (1, 3, 2):
                dst = rows16((4 - d) // 2 if first[h] == "x" else (4 - d) * 2)
                send(ref.at[0, rows16(0), cols[h]], ref.at[d % 2, dst, cols[h]], "gather", (name, "a", h), along(first[h], d))

    def gather_first_end(ref, name):
        for h in halves:
            arrived(ref.at[0, pl.ds(0, 3 * ROWS), cols[h]], (name, "a", h))

    def gather_second(ref, name, r):
        q = chunk[r]
        for d in (1, 3, 2):
            there = lax.rem(q + d, 2)
            send(
                ref.at[q, pl.ds(0, PAIR), cols[0]], ref.at[there, pl.ds((4 - d) * PAIR, PAIR), cols[0]],
                "gather", (name, "b", r), along(second[0], d),
            )
            for e in (0, 2):
                send(
                    ref.at[q, rows16((q + e) * 2), cols[1]], ref.at[there, rows16((q + e) * 2 + (4 - d) // 2), cols[1]],
                    "gather", (name, "b", r), along(second[1], d),
                )

    def gather_end(ref, name, r):
        arrived(ref.at[0, pl.ds(0, 3 * PAIR)], (name, "b", r))

    def share(dz):
        return rows16(lax.rem(z + dz, NZ))

    def reduce_step(n, r, t):
        if t > 1:
            arrived(zrcv.at[n, r, 0, 0] if t == 2 else zrcv.at[n, r, t - 2], ("r", n, r, t - 1))
        for way, dev in ((0, z_up), (1, z_down)):
            dz = 5 - t if way == 0 else 3 + t
            near, far = (mine, theirs) if way == 0 else (theirs, mine)
            buf, dst = zsnd.at[n, r, t - 1, way], zrcv.at[n, r, t - 1, way]
            if t == 1:
                buf[:, near] = part[n, r, share(dz), near].astype(BF16)
                buf, dst = buf.at[:, near], dst.at[:, near]
            elif t == 2:
                buf[:, near] = (part[n, r, share(dz), near] + zrcv[n, r, 0, way, :, near].astype(F32)).astype(BF16)
                buf[:, far] = part[n, r, share(dz), far].astype(BF16)
            else:
                buf[...] = (part[n, r, share(dz)] + zrcv[n, r, t - 2, way].astype(F32)).astype(BF16)
            send(buf, dst, ("z", n), ("r", n, r, t), dev)

    def reduce_end(n, r):
        arrived(zrcv.at[n, r, 3], ("r", n, r, 4))
        return part[n, r, share(0)] + zrcv[n, r, 3, 0].astype(F32) + zrcv[n, r, 3, 1].astype(F32)

    def spread_step(n, r, t):
        ref = grd if n else act
        if t > 1:
            arrived(zrcv.at[n, r, 3], ("s", n, r, t - 1))
        for way, dev in ((0, z_up), (1, z_down)):
            piece = ref.at[chunk[r], share(NZ + 1 - t if way == 0 else t - 1)]
            if t == 4:
                piece = piece.at[:, theirs if way else mine]
            send(piece, piece, ("z", n), ("s", n, r, t), dev)

    def spread_end(n, r):
        arrived(zrcv.at[n, r, 3, 0], ("s", n, r, 4))
        ref, dst = (grd, grd2) if n else (act, act2)
        send(ref.at[chunk[r], :, theirs], dst.at[chunk[r]], "near", ("near", n), sibling)

    def scatter_first(n, r, h, value):
        if h == 1:
            tmp[...] = value
        for d in (2, 1, 3, 0):
            if h == 0:
                val = value[d * PAIR : (d + 1) * PAIR]
            else:
                f = lax.rem(chunk[r] + d, 2)
                val = jnp.concatenate([tmp[rows16((f + e) * 2 + d // 2)] for e in (0, 2)], axis=0)
            if d == 0:
                own[n, r, h] = val
            else:
                lsnd[n, r, h, d - 1] = val.astype(BF16)
                send(lsnd.at[n, r, h, d - 1], lrcv.at[n, r, h, d - 1], ("l", n), ("l", n, r, h), along(second[h], d))

    def scatter_second(n, r):
        q = chunk[r]
        for h in halves:
            arrived(lrcv.at[n, r, h], ("l", n, r, h))
            got = [lrcv[n, r, h, d].astype(F32) for d in (0, 1, 2)]
            ssnd[n, r, h] = own[n, r, h] + got[0] + got[1] + got[2]
            send(ssnd.at[n, r, h, rows16(1)], srcv.at[n, h, q + 1], ("l", n), ("m", n, h), along(first[h], q + 2))

            @pl.when(q == 1)
            def _():
                send(ssnd.at[n, r, h, rows16(0)], srcv.at[n, h, 0], ("l", n), ("m", n, h), along(first[h], 1), r == 0)

    def scatter_end(n, ref):
        for h in halves:
            arrived(srcv.at[n, h], ("m", n, h))
            total = ssnd[n, parity, h, rows16(0)] + srcv[n, h, 0] + srcv[n, h, 1] + srcv[n, h, 2]
            ref[:, cols[h]] = total.astype(BF16)

    def multiply(n, r):
        if n == 0:
            part[0, r] = mm(tok[chunk[r]], wi[...])
        else:
            part[1, r] = mm(cot[chunk[r]], wot[...])
        reduce_step(n, r, 1)

    def middle(n, r):
        total = reduce_end(n, r)
        if n == 0:
            gelu_out, derivative = activate(total)
            act[chunk[r], share(0)] = gelu_out.astype(BF16)
            slope[r] = derivative
        else:
            grd[chunk[r], share(0)] = (total * slope[r]).astype(BF16)
        spread_step(n, r, 1)

    def finish(n, r):
        spread_end(n, r)
        for h in halves:
            if n == 0:
                scatter_first(n, r, h, mm(act[chunk[r]], wo[:, cols[h]]))
            else:
                scatter_first(n, r, h, mm(grd[chunk[r]], wit[:, cols[h]]))

    def both(ref, first_chunk):
        got = ref[pl.ds(first_chunk, 2)]
        return got.reshape(-1, got.shape[-1])

    def weight_grad(n):
        if n == 0:
            arrived(cot.at[pl.ds(2, 2)], "cot2")
            arrived(act2, ("near", 0))
            total = mm_tn(act[:, :, mine].reshape(MINE, HID), both(cot, 0)) + mm_tn(both(act2, 0), both(cot, 2))
            gwo[...] = total.astype(BF16)
        else:
            arrived(tok.at[pl.ds(2, 2)], "tok2")
            arrived(grd2, ("near", 1))
            total = mm_tn(both(tok, 0), grd[:, :, mine].reshape(MINE, HID)) + mm_tn(both(tok, 2), both(grd2, 0))
            gwi[...] = total.astype(BF16)

    got_tok.wait()
    gather_first(tok, "tok")
    got_wi.wait()
    send(wi.at[:, mine], wi.at[:, theirs], "wi", "wi", sibling)
    got_cot.wait()
    gather_first(cot, "cot")
    got_wo.wait()
    for i in range(3):
        wot[:, pl.ds(i * 256, 256)] = wo[pl.ds(i * 256, 256)].T
    send(wot.at[:, mine], wot.at[:, theirs], "wot", "wot", sibling)
    gather_first_end(tok, "tok")
    gather_second(tok, "tok", 0)
    gather_second(tok, "tok", 1)
    for i in range(3):
        wit[pl.ds(i * 256, 256)] = wi[:, pl.ds(i * 256, 256)].T
    send(wo.at[mine], wo.at[theirs], "wo", "wo", sibling)
    send(wit.at[mine], wit.at[theirs], "wit", "wit", sibling)
    gather_first_end(cot, "cot")
    gather_end(tok, "tok", 0)
    gather_second(cot, "cot", 0)
    arrived(wi.at[:, theirs], "wi")
    multiply(0, 0)
    gather_end(tok, "tok", 1)
    gather_second(cot, "cot", 1)
    multiply(0, 1)
    reduce_step(0, 0, 2)
    gather_end(cot, "cot", 0)
    arrived(wot.at[:, theirs], "wot")
    multiply(1, 0)
    reduce_step(0, 1, 2)
    gather_end(cot, "cot", 1)
    multiply(1, 1)
    send(tok.at[pl.ds(0, 2)], tok.at[pl.ds(2, 2)], "near", "tok2", sibling)
    send(cot.at[pl.ds(0, 2)], cot.at[pl.ds(2, 2)], "near", "cot2", sibling)
    reduce_step(0, 0, 3)
    reduce_step(1, 0, 2)
    reduce_step(0, 1, 3)
    reduce_step(1, 1, 2)
    reduce_step(0, 0, 4)
    reduce_step(1, 0, 3)
    reduce_step(0, 1, 4)
    reduce_step(1, 1, 3)
    middle(0, 0)
    reduce_step(1, 0, 4)
    middle(0, 1)
    reduce_step(1, 1, 4)
    spread_step(0, 0, 2)
    middle(1, 0)
    spread_step(0, 1, 2)
    middle(1, 1)
    spread_step(0, 0, 3)
    spread_step(1, 0, 2)
    spread_step(0, 1, 3)
    spread_step(1, 1, 2)
    spread_step(0, 0, 4)
    spread_step(1, 0, 3)
    spread_step(0, 1, 4)
    spread_step(1, 1, 3)
    arrived(wo.at[theirs], "wo")
    finish(0, 0)
    spread_step(1, 0, 4)
    finish(0, 1)
    spread_step(1, 1, 4)
    arrived(wit.at[theirs], "wit")
    finish(1, 0)
    scatter_second(0, 0)
    finish(1, 1)
    scatter_second(0, 1)
    weight_grad(0)
    scatter_second(1, 0)
    weight_grad(1)
    scatter_second(1, 1)
    scatter_end(0, out_ref)
    scatter_end(1, gt_ref)
    for s in sent:
        all_sent(s)
    for pool, known in ((ssem, N_SEND), (rsem, N_RECV), (lsem, 4)):
        assert len(names[id(pool)]) <= known, len(names[id(pool)])


def hand_over(*refs):
    srcs, dsts, sems = refs[:4], refs[4:8], refs[8]
    copies = []
    for s, d in zip(srcs, dsts):
        parts = s.shape[0] // 192 or 1
        for p in range(parts):
            rows = pl.ds(p * (s.shape[0] // parts), s.shape[0] // parts)
            copies.append(pltpu.make_async_copy(s.at[rows], d.at[rows], sems.at[len(copies)]))
    for copy in copies:
        copy.start()
    for copy in copies:
        copy.wait()


def per_device(tokens, weight_in, weight_out, cotangent):
    hbm = pl.BlockSpec(memory_space=pltpu.HBM)
    vmem = pl.BlockSpec(memory_space=pltpu.VMEM)
    shape = jax.ShapeDtypeStruct
    shapes = (
        shape((ROWS, FEAT), BF16), shape((ROWS, FEAT), BF16), shape((FEAT, HID), BF16), shape((HID, FEAT), BF16),
    )
    tokens, cotangent = [pltpu.with_memory_space_constraint(a, pltpu.HBM) for a in (tokens, cotangent)]
    results = pl.pallas_call(
        kernel,
        out_shape=shapes,
        in_specs=[hbm] * 4,
        out_specs=(vmem,) * 4,
        scratch_shapes=[
            pltpu.VMEM((FEAT, 2 * HID), BF16),
            pltpu.VMEM((2 * HID, FEAT), BF16),
            pltpu.VMEM((2 * HID, FEAT), BF16),
            pltpu.VMEM((FEAT, 2 * HID), BF16),
            pltpu.VMEM((4, CHUNK, FEAT), BF16),
            pltpu.VMEM((4, CHUNK, FEAT), BF16),
            pltpu.VMEM((2, 2, CHUNK, 2 * HID), F32),
            pltpu.VMEM((2, 2, 4, 2, ROWS, 2 * HID), BF16),
            pltpu.VMEM((2, 2, 4, 2, ROWS, 2 * HID), BF16),
            pltpu.VMEM((2, CHUNK, 2 * HID), BF16),
            pltpu.VMEM((2, CHUNK, 2 * HID), BF16),
            pltpu.VMEM((2, CHUNK, HID), BF16),
            pltpu.VMEM((2, CHUNK, HID), BF16),
            pltpu.VMEM((2, ROWS, 2 * HID), F32),
            pltpu.VMEM((CHUNK, FH), F32),
            pltpu.VMEM((2, 2, 2, PAIR, FH), F32),
            pltpu.VMEM((2, 2, 2, 3, PAIR, FH), BF16),
            pltpu.VMEM((2, 2, 2, 3, PAIR, FH), BF16),
            pltpu.VMEM((2, 2, 2, PAIR, FH), F32),
            pltpu.VMEM((2, 2, 3, ROWS, FH), F32),
            pltpu.SemaphoreType.DMA((N_SEND,)),
            pltpu.SemaphoreType.DMA((N_RECV,)),
            pltpu.SemaphoreType.DMA((4,)),
        ],
        compiler_params=pltpu.CompilerParams(
            collective_id=0, has_side_effects=True, vmem_limit_bytes=48 * 2**20
        ),
        cost_estimate=pl.CostEstimate(flops=7 * 10**9, bytes_accessed=10**7, transcendentals=5 * 10**4),
    )(tokens, weight_in, weight_out, cotangent)
    return pl.pallas_call(
        hand_over,
        out_shape=shapes,
        in_specs=[vmem] * 4,
        out_specs=(hbm,) * 4,
        scratch_shapes=[pltpu.SemaphoreType.DMA((14,))],
        compiler_params=pltpu.CompilerParams(vmem_limit_bytes=2**21),
        cost_estimate=pl.CostEstimate(flops=0, bytes_accessed=10**7, transcendentals=0),
    )(*results)


def solution(mesh):
    in_specs = (P("row", "col"), P("col", "row"), P("row", "col"), P("row", "col"))
    out_specs = (P("row", "col"), P("row", "col"), P("col", "row"), P("row", "col"))
    return jax.shard_map(
        per_device, mesh=mesh, in_specs=in_specs, out_specs=out_specs, check_vma=False
    )
```

```python
import jax
import jax.numpy as jnp
from jax import lax
from jax.experimental import pallas as pl
from jax.experimental.pallas import tpu as pltpu
from jax.sharding import PartitionSpec as P

MESH = pl.DeviceIdType.MESH
F32, BF16 = jnp.float32, jnp.bfloat16
gelu_scale = 0.7978845608028654
gelu_cubic = 0.044715

NZ = 8
NX = NY = 4
ROWS = 16
MINE = NY * NX * ROWS
CHUNK = MINE // 2
PAIR = 2 * ROWS
FEAT = 1536
FH = FEAT // 2
HID = 768
N_SEND, N_RECV = 10, 56


def activate(hidden):
    tangent = jnp.tanh(gelu_scale * (hidden + gelu_cubic * hidden * hidden * hidden))
    gelu_out = 0.5 * hidden * (1.0 + tangent)
    derivative = 0.5 * (1.0 + tangent) + 0.5 * hidden * (1.0 - tangent * tangent) * gelu_scale * (
        1.0 + 3.0 * gelu_cubic * hidden * hidden
    )
    return (gelu_out, derivative)


def mm(left, right):
    return lax.dot_general(left, right, (((1,), (0,)), ((), ())), preferred_element_type=F32)


def mm_tn(left, right):
    return lax.dot_general(left, right, (((0,), (0,)), ((), ())), preferred_element_type=F32)


def kernel(
    tok_hbm, wi_hbm, wo_hbm, cot_hbm,
    out_ref, gt_ref, gwi, gwo,
    wi, wo, wit, wot, tok, cot, part, zsnd, zrcv, act, grd, act2, grd2, slope, lsnd, lrcv, ssnd, srcv,
    ssem, rsem, lsem,
):
    row, z = lax.axis_index("row"), lax.axis_index("col")
    c, x, y = lax.rem(row, 2), lax.rem(row // 2, NX), row // (2 * NX)
    parity = lax.rem(x + y, 2)
    stages = halves = (0, 1)
    chunk = [lax.rem(r + parity, 2) for r in stages]

    def at(cc, dy, dx, dz):
        return ((lax.rem(y + dy, NY) * NX + lax.rem(x + dx, NX)) * 2 + cc, lax.rem(z + dz, NZ))

    def along(axis, d):
        return at(c, d, 0, 0) if axis == "y" else at(c, 0, d, 0)

    sibling, z_up, z_down = at(1 - c, 0, 0, 0), at(c, 0, 0, 1), at(c, 0, 0, NZ - 1)
    z_up2, z_down2 = at(c, 0, 0, 2), at(c, 0, 0, NZ - 2)

    names = {}

    def sem(pool, name):
        known = names.setdefault(id(pool), {})
        return pool.at[known.setdefault(name, len(known))]

    def copy_to(src, dst, s, r, dev):
        return pltpu.make_async_remote_copy(
            src_ref=src, dst_ref=dst, send_sem=sem(ssem, s), recv_sem=sem(rsem, r),
            device_id=dev, device_id_type=MESH,
        )

    sent = {}

    def send(src, dst, s, r, dev, counts=True):
        copy_to(src, dst, s, r, dev).start()
        size = src.dtype.itemsize if counts else 0
        for n in src.shape:
            size *= n
        sent[s] = sent.get(s, 0) + size

    def arrived(like, r):
        copy_to(like, like, "wi", r, sibling).wait_recv()

    def all_sent(s):
        n = sent[s] // (HID * 2)
        assert n * HID * 2 == sent[s] and n <= FEAT, (s, n)
        like = wi.at[pl.ds(0, n), pl.ds(0, HID)]
        copy_to(like, like, s, "wi", sibling).wait_send()

    def fetch(src, dst, name):
        copy = pltpu.make_async_copy(src, dst, sem(lsem, name))
        copy.start()
        return copy

    def rows16(i):
        return pl.ds(i * ROWS if isinstance(i, int) else pl.multiple_of(i * ROWS, ROWS), ROWS)

    mine, theirs = pl.ds(0, HID), pl.ds(HID, HID)

    got_tok = fetch(tok_hbm, tok.at[0, rows16(0)], "tok")
    got_cot = fetch(cot_hbm, cot.at[0, rows16(0)], "cot")
    got_wi = fetch(wi_hbm, wi.at[:, mine], "wi")
    got_wo = fetch(wo_hbm, wo.at[mine], "wo")

    barrier = pltpu.get_barrier_semaphore()
    partners = [sibling, z_up, z_down, z_up2, z_down2] + [along(a, d) for a in ("x", "y") for d in (1, 2, 3)]
    for dev in partners:
        pl.semaphore_signal(barrier, inc=1, device_id=dev, device_id_type=MESH)
    pl.semaphore_wait(barrier, len(partners))

    first, second = ("x", "y"), ("y", "x")
    cols = [pl.ds(h * FH, FH) for h in halves]

    def gather_first(ref, name):
        for h in halves:
            for d in (1, 3, 2):
                dst = rows16((4 - d) // 2 if first[h] == "x" else (4 - d) * 2)
                send(ref.at[0, rows16(0), cols[h]], ref.at[d % 2, dst, cols[h]], "gather", (name, "a", h), along(first[h], d))

    def gather_first_end(ref, name):
        for h in halves:
            arrived(ref.at[0, pl.ds(0, 3 * ROWS), cols[h]], (name, "a", h))

    def gather_second(ref, name, r):
        q = chunk[r]
        for d in (1, 3, 2):
            there = lax.rem(q + d, 2)
            send(
                ref.at[q, pl.ds(0, PAIR), cols[0]], ref.at[there, pl.ds((4 - d) * PAIR, PAIR), cols[0]],
                "gather", (name, "b", r), along(second[0], d),
            )
            for e in (0, 2):
                send(
                    ref.at[q, rows16((q + e) * 2), cols[1]], ref.at[there, rows16((q + e) * 2 + (4 - d) // 2), cols[1]],
                    "gather", (name, "b", r), along(second[1], d),
                )

    def gather_end(ref, name, r):
        arrived(ref.at[0, pl.ds(0, 3 * PAIR)], (name, "b", r))

    def share(dz):
        return rows16(lax.rem(z + dz, NZ))

    def reduce_step(n, r, t):
        if t == 3 and n == 0:
            arrived(tok.at[0, pl.ds(0, 3 * ROWS)], ("r", n, r, 1))
        elif t > 1:
            arrived(zrcv.at[n, r, 0, 0] if t == 2 else zrcv.at[n, r, t - 2], ("r", n, r, t - 1))
        for way, dev, dev2 in ((0, z_up, z_up2), (1, z_down, z_down2)):
            dz = 5 - t if way == 0 else 3 + t
            near = mine if way == 0 else theirs
            buf, dst = zsnd.at[n, r, t - 1, way], zrcv.at[n, r, t - 1, way]
            if t == 1:
                buf[:, near] = part[n, r, share(dz), near].astype(BF16)
                buf, dst = buf.at[:, near], dst.at[:, near]
                if n == 0:
                    send(buf, dst, ("z", n), ("r", n, r, 1), dev2)
                    buf, dst = zsnd.at[n, r, 1, way], zrcv.at[n, r, 1, way]
                    buf[...] = part[n, r, share(3 if way == 0 else 5)].astype(BF16)
            elif t == 2 or (t == 3 and n == 0):
                there = zrcv[n, r, 1, way].astype(F32) if n == 0 else 0.0
                total = part[n, r, share(dz)] + there
                a, b = total[:, : HID], total[:, HID:]
                extra = zrcv[n, r, 0, way, :, near].astype(F32)
                a, b = (a + extra, b) if way == 0 else (a, b + extra)
                buf[:, mine] = a.astype(BF16)
                buf[:, theirs] = b.astype(BF16)
            else:
                buf[...] = (part[n, r, share(dz)] + zrcv[n, r, t - 2, way].astype(F32)).astype(BF16)
            send(buf, dst, ("z", n), ("r", n, r, t), dev)

    def reduce_end(n, r):
        arrived(zrcv.at[n, r, 3], ("r", n, r, 4))
        return part[n, r, share(0)] + zrcv[n, r, 3, 0].astype(F32) + zrcv[n, r, 3, 1].astype(F32)

    def spread_step(n, r, t):
        ref = grd if n else act
        if t > 1:
            arrived(zrcv.at[n, r, 3], ("s", n, r, t - 1))
        for way, dev in ((0, z_up), (1, z_down)):
            dz = NZ + 1 - t if way == 0 else t - 1
            piece = ref.at[chunk[r], share(dz)]
            near = theirs if way else mine
            if t == 3 and n == 1:
                send(piece.at[:, near], piece.at[:, near], ("z", n), ("s", n, r, t), z_down2 if way else z_up2)
            if t == 4:
                piece = piece.at[:, near]
            send(piece, piece, ("z", n), ("s", n, r, t), dev)
        for dz in (0,) if t == 1 else (NZ + 1 - t, t - 1):
            hand_near(n, r, dz)

    def spread_end(n, r):
        if n == 0:
            arrived(zrcv.at[n, r, 3, 0], ("s", n, r, 4))
        else:
            arrived(tok.at[0, pl.ds(0, 3 * ROWS)], ("s", n, r, 3))
            hand_near(n, r, 3)
            hand_near(n, r, 5)
        hand_near(n, r, 4)

    def hand_near(n, r, dz):
        ref, dst = (grd, grd2) if n else (act, act2)
        send(ref.at[chunk[r], share(dz), theirs], dst.at[chunk[r], share(dz)], "near", ("near", n), sibling)

    def scatter_first(n, r, h):
        for d in (2, 1, 3):
            if h == 0:
                lsnd[n, r, h, d - 1] = part[n, r, pl.ds(d * PAIR, PAIR), cols[h]].astype(BF16)
            else:
                f = lax.rem(chunk[r] + d, 2)
                for i, e in enumerate((0, 2)):
                    lsnd[n, r, h, d - 1, rows16(i)] = part[n, r, rows16((f + e) * 2 + d // 2), cols[h]].astype(BF16)
            send(lsnd.at[n, r, h, d - 1], lrcv.at[n, r, h, d - 1], ("l", n), ("l", n, r, h), along(second[h], d))

    def scatter_second(n, r):
        q = chunk[r]
        for h in halves:
            arrived(lrcv.at[n, r, h], ("l", n, r, h))
            got = [lrcv[n, r, h, d].astype(F32) for d in (0, 1, 2)]
            if h == 0:
                own = part[n, r, pl.ds(0, PAIR), cols[h]]
            else:
                own = jnp.concatenate([part[n, r, rows16((q + e) * 2), cols[h]] for e in (0, 2)], axis=0)
            ssnd[n, r, h] = own + got[0] + got[1] + got[2]
            send(ssnd.at[n, r, h, rows16(1)], srcv.at[n, h, q + 1], ("l", n), ("m", n, h), along(first[h], q + 2))

            @pl.when(q == 1)
            def _():
                send(ssnd.at[n, r, h, rows16(0)], srcv.at[n, h, 0], ("l", n), ("m", n, h), along(first[h], 1), r == 0)

    def scatter_end(n, ref):
        for h in halves:
            arrived(srcv.at[n, h], ("m", n, h))
            total = ssnd[n, parity, h, rows16(0)] + srcv[n, h, 0] + srcv[n, h, 1] + srcv[n, h, 2]
            ref[:, cols[h]] = total.astype(BF16)

    def multiply(n, r):
        if n == 0:
            part[0, r] = mm(tok[chunk[r]], wi[...])
        else:
            part[1, r] = mm(cot[chunk[r]], wot[...])
        reduce_step(n, r, 1)

    def middle(n, r):
        total = reduce_end(n, r)
        if n == 0:
            gelu_out, derivative = activate(total)
            act[chunk[r], share(0)] = gelu_out.astype(BF16)
            slope[r] = derivative
        else:
            grd[chunk[r], share(0)] = (total * slope[r]).astype(BF16)
        spread_step(n, r, 1)

    def finish(n, r):
        spread_end(n, r)
        for h in halves:
            if n == 0:
                part[n, r, :, cols[h]] = mm(act[chunk[r]], wo[:, cols[h]])
            else:
                part[n, r, :, cols[h]] = mm(grd[chunk[r]], wit[:, cols[h]])
            scatter_first(n, r, h)

    def both(ref, first_chunk):
        got = ref[pl.ds(first_chunk, 2)]
        return got.reshape(-1, got.shape[-1])

    def weight_grad(n):
        if n == 0:
            arrived(cot.at[pl.ds(2, 2)], "cot2")
            arrived(act2, ("near", 0))
            total = mm_tn(act[:, :, mine].reshape(MINE, HID), both(cot, 0)) + mm_tn(both(act2, 0), both(cot, 2))
            gwo[...] = total.astype(BF16)
        else:
            arrived(tok.at[pl.ds(2, 2)], "tok2")
            arrived(grd2, ("near", 1))
            total = mm_tn(both(tok, 0), grd[:, :, mine].reshape(MINE, HID)) + mm_tn(both(tok, 2), both(grd2, 0))
            gwi[...] = total.astype(BF16)

    got_tok.wait()
    gather_first(tok, "tok")
    got_wi.wait()
    send(wi.at[:, mine], wi.at[:, theirs], "wi", "wi", sibling)
    got_cot.wait()
    gather_first(cot, "cot")
    got_wo.wait()
    for i in range(3):
        wot[:, pl.ds(i * 256, 256)] = wo[pl.ds(i * 256, 256)].T
    send(wot.at[:, mine], wot.at[:, theirs], "wot", "wot", sibling)
    gather_first_end(tok, "tok")
    gather_second(tok, "tok", 0)
    gather_second(tok, "tok", 1)
    for i in range(3):
        wit[pl.ds(i * 256, 256)] = wi[:, pl.ds(i * 256, 256)].T
    send(wo.at[mine], wo.at[theirs], "wo", "wo", sibling)
    send(wit.at[mine], wit.at[theirs], "wit", "wit", sibling)
    gather_first_end(cot, "cot")
    gather_end(tok, "tok", 0)
    gather_second(cot, "cot", 0)
    arrived(wi.at[:, theirs], "wi")
    multiply(0, 0)
    gather_end(tok, "tok", 1)
    gather_second(cot, "cot", 1)
    multiply(0, 1)
    gather_end(cot, "cot", 0)
    arrived(wot.at[:, theirs], "wot")
    multiply(1, 0)
    reduce_step(0, 0, 3)
    gather_end(cot, "cot", 1)
    multiply(1, 1)
    send(tok.at[pl.ds(0, 2)], tok.at[pl.ds(2, 2)], "near", "tok2", sibling)
    send(cot.at[pl.ds(0, 2)], cot.at[pl.ds(2, 2)], "near", "cot2", sibling)
    reduce_step(0, 1, 3)
    reduce_step(1, 0, 2)
    reduce_step(0, 0, 4)
    reduce_step(1, 1, 2)
    reduce_step(0, 1, 4)
    reduce_step(1, 0, 3)
    middle(0, 0)
    reduce_step(1, 1, 3)
    middle(0, 1)
    reduce_step(1, 0, 4)
    spread_step(0, 0, 2)
    reduce_step(1, 1, 4)
    spread_step(0, 1, 2)
    middle(1, 0)
    spread_step(0, 0, 3)
    middle(1, 1)
    spread_step(0, 1, 3)
    spread_step(1, 0, 2)
    spread_step(0, 0, 4)
    spread_step(1, 1, 2)
    spread_step(0, 1, 4)
    spread_step(1, 0, 3)
    arrived(wo.at[theirs], "wo")
    finish(0, 0)
    spread_step(1, 1, 3)
    finish(0, 1)
    arrived(wit.at[theirs], "wit")
    finish(1, 0)
    scatter_second(0, 0)
    finish(1, 1)
    scatter_second(0, 1)
    weight_grad(0)
    scatter_second(1, 0)
    weight_grad(1)
    scatter_second(1, 1)
    scatter_end(0, out_ref)
    scatter_end(1, gt_ref)
    for s in sent:
        all_sent(s)
    for pool, known in ((ssem, N_SEND), (rsem, N_RECV), (lsem, 4)):
        assert len(names[id(pool)]) <= known, len(names[id(pool)])


def hand_over(*refs):
    srcs, dsts, sems = refs[:4], refs[4:8], refs[8]
    copies = []
    for s, d in zip(srcs, dsts):
        parts = s.shape[0] // 192 or 1
        for p in range(parts):
            rows = pl.ds(p * (s.shape[0] // parts), s.shape[0] // parts)
            copies.append(pltpu.make_async_copy(s.at[rows], d.at[rows], sems.at[len(copies)]))
    for copy in copies:
        copy.start()
    for copy in copies:
        copy.wait()


def per_device(tokens, weight_in, weight_out, cotangent):
    hbm = pl.BlockSpec(memory_space=pltpu.HBM)
    vmem = pl.BlockSpec(memory_space=pltpu.VMEM)
    shape = jax.ShapeDtypeStruct
    shapes = (
        shape((ROWS, FEAT), BF16), shape((ROWS, FEAT), BF16), shape((FEAT, HID), BF16), shape((HID, FEAT), BF16),
    )
    tokens, cotangent = [pltpu.with_memory_space_constraint(a, pltpu.HBM) for a in (tokens, cotangent)]
    results = pl.pallas_call(
        kernel,
        out_shape=shapes,
        in_specs=[hbm] * 4,
        out_specs=(vmem,) * 4,
        scratch_shapes=[
            pltpu.VMEM((FEAT, 2 * HID), BF16),
            pltpu.VMEM((2 * HID, FEAT), BF16),
            pltpu.VMEM((2 * HID, FEAT), BF16),
            pltpu.VMEM((FEAT, 2 * HID), BF16),
            pltpu.VMEM((4, CHUNK, FEAT), BF16),
            pltpu.VMEM((4, CHUNK, FEAT), BF16),
            pltpu.VMEM((2, 2, CHUNK, 2 * HID), F32),
            pltpu.VMEM((2, 2, 4, 2, ROWS, 2 * HID), BF16),
            pltpu.VMEM((2, 2, 4, 2, ROWS, 2 * HID), BF16),
            pltpu.VMEM((2, CHUNK, 2 * HID), BF16),
            pltpu.VMEM((2, CHUNK, 2 * HID), BF16),
            pltpu.VMEM((2, CHUNK, HID), BF16),
            pltpu.VMEM((2, CHUNK, HID), BF16),
            pltpu.VMEM((2, ROWS, 2 * HID), F32),
            pltpu.VMEM((2, 2, 2, 3, PAIR, FH), BF16),
            pltpu.VMEM((2, 2, 2, 3, PAIR, FH), BF16),
            pltpu.VMEM((2, 2, 2, PAIR, FH), F32),
            pltpu.VMEM((2, 2, 3, ROWS, FH), F32),
            pltpu.SemaphoreType.DMA((N_SEND,)),
            pltpu.SemaphoreType.DMA((N_RECV,)),
            pltpu.SemaphoreType.DMA((4,)),
        ],
        compiler_params=pltpu.CompilerParams(
            collective_id=0, has_side_effects=True, vmem_limit_bytes=48 * 2**20
        ),
        cost_estimate=pl.CostEstimate(flops=7 * 10**9, bytes_accessed=10**7, transcendentals=5 * 10**4),
    )(tokens, weight_in, weight_out, cotangent)
    return pl.pallas_call(
        hand_over,
        out_shape=shapes,
        in_specs=[vmem] * 4,
        out_specs=(hbm,) * 4,
        scratch_shapes=[pltpu.SemaphoreType.DMA((14,))],
        compiler_params=pltpu.CompilerParams(vmem_limit_bytes=2**21),
        cost_estimate=pl.CostEstimate(flops=0, bytes_accessed=10**7, transcendentals=0),
    )(*results)


def solution(mesh):
    in_specs = (P("row", "col"), P("col", "row"), P("row", "col"), P("row", "col"))
    out_specs = (P("row", "col"), P("row", "col"), P("col", "row"), P("row", "col"))
    return jax.shard_map(
        per_device, mesh=mesh, in_specs=in_specs, out_specs=out_specs, check_vma=False
    )
```

```python
import jax
import jax.numpy as jnp
from jax import lax
from jax.experimental import pallas as pl
from jax.experimental.pallas import tpu as pltpu
from jax.sharding import PartitionSpec as P

MESH = pl.DeviceIdType.MESH
F32, BF16 = jnp.float32, jnp.bfloat16
gelu_scale = 0.7978845608028654
gelu_cubic = 0.044715

NZ = 8
NX = NY = 4
ROWS = 16
MINE = NY * NX * ROWS
CHUNK = MINE // 2
PAIR = 2 * ROWS
FEAT = 1536
FH = FEAT // 2
HID = 768
N_SEND, N_RECV = 10, 56


def activate(hidden):
    tangent = jnp.tanh(gelu_scale * (hidden + gelu_cubic * hidden * hidden * hidden))
    gelu_out = 0.5 * hidden * (1.0 + tangent)
    derivative = 0.5 * (1.0 + tangent) + 0.5 * hidden * (1.0 - tangent * tangent) * gelu_scale * (
        1.0 + 3.0 * gelu_cubic * hidden * hidden
    )
    return (gelu_out, derivative)


def mm(left, right):
    return lax.dot_general(left, right, (((1,), (0,)), ((), ())), preferred_element_type=F32)


def mm_tn(left, right):
    return lax.dot_general(left, right, (((0,), (0,)), ((), ())), preferred_element_type=F32)


def kernel(
    tok_hbm, wi_hbm, wo_hbm, cot_hbm,
    out_ref, gt_ref, gwi, gwo,
    wi, wo, wit, wot, tok, cot, part, zsnd, zrcv, act, grd, act2, grd2, slope, lsnd, lrcv, ssnd, srcv,
    ssem, rsem, lsem,
):
    row, z = lax.axis_index("row"), lax.axis_index("col")
    c, x, y = lax.rem(row, 2), lax.rem(row // 2, NX), row // (2 * NX)
    parity = lax.rem(x + y, 2)
    stages = halves = (0, 1)
    chunk = [lax.rem(r + parity, 2) for r in stages]

    def at(cc, dy, dx, dz):
        return ((lax.rem(y + dy, NY) * NX + lax.rem(x + dx, NX)) * 2 + cc, lax.rem(z + dz, NZ))

    def along(axis, d):
        return at(c, d, 0, 0) if axis == "y" else at(c, 0, d, 0)

    sibling, z_up, z_down = at(1 - c, 0, 0, 0), at(c, 0, 0, 1), at(c, 0, 0, NZ - 1)
    z_up2, z_down2 = at(c, 0, 0, 2), at(c, 0, 0, NZ - 2)

    names = {}

    def sem(pool, name):
        known = names.setdefault(id(pool), {})
        return pool.at[known.setdefault(name, len(known))]

    def copy_to(src, dst, s, r, dev):
        return pltpu.make_async_remote_copy(
            src_ref=src, dst_ref=dst, send_sem=sem(ssem, s), recv_sem=sem(rsem, r),
            device_id=dev, device_id_type=MESH,
        )

    sent = {}

    def send(src, dst, s, r, dev, counts=True):
        copy_to(src, dst, s, r, dev).start()
        size = src.dtype.itemsize if counts else 0
        for n in src.shape:
            size *= n
        sent[s] = sent.get(s, 0) + size

    def arrived(like, r):
        copy_to(like, like, "wi", r, sibling).wait_recv()

    def all_sent(s):
        n = sent[s] // (HID * 2)
        assert n * HID * 2 == sent[s] and n <= FEAT, (s, n)
        like = wi.at[pl.ds(0, n), pl.ds(0, HID)]
        copy_to(like, like, s, "wi", sibling).wait_send()

    def fetch(src, dst, name):
        copy = pltpu.make_async_copy(src, dst, sem(lsem, name))
        copy.start()
        return copy

    def rows16(i):
        return pl.ds(i * ROWS if isinstance(i, int) else pl.multiple_of(i * ROWS, ROWS), ROWS)

    mine, theirs = pl.ds(0, HID), pl.ds(HID, HID)

    got_tok = fetch(tok_hbm, tok.at[0, rows16(0)], "tok")
    got_cot = fetch(cot_hbm, cot.at[0, rows16(0)], "cot")
    got_wi = fetch(wi_hbm, wi.at[:, mine], "wi")
    got_wo = fetch(wo_hbm, wo.at[mine], "wo")

    barrier = pltpu.get_barrier_semaphore()
    partners = [sibling, z_up, z_down, z_up2, z_down2] + [along(a, d) for a in ("x", "y") for d in (1, 2, 3)]
    for dev in partners:
        pl.semaphore_signal(barrier, inc=1, device_id=dev, device_id_type=MESH)
    pl.semaphore_wait(barrier, len(partners))

    first, second = ("x", "y"), ("y", "x")
    cols = [pl.ds(h * FH, FH) for h in halves]

    def gather_first(ref, name):
        for h in halves:
            for d in (2, 1, 3):
                dst = rows16((4 - d) // 2 if first[h] == "x" else (4 - d) * 2)
                send(ref.at[0, rows16(0), cols[h]], ref.at[d % 2, dst, cols[h]], "gather", (name, "a", h), along(first[h], d))

    def gather_first_end(ref, name):
        for h in halves:
            arrived(ref.at[0, pl.ds(0, 3 * ROWS), cols[h]], (name, "a", h))

    def gather_second(ref, name, r):
        q = chunk[r]
        for d in (2, 1, 3):
            there = lax.rem(q + d, 2)
            send(
                ref.at[q, pl.ds(0, PAIR), cols[0]], ref.at[there, pl.ds((4 - d) * PAIR, PAIR), cols[0]],
                "gather", (name, "b", r), along(second[0], d),
            )
            for e in (0, 2):
                send(
                    ref.at[q, rows16((q + e) * 2), cols[1]], ref.at[there, rows16((q + e) * 2 + (4 - d) // 2), cols[1]],
                    "gather", (name, "b", r), along(second[1], d),
                )

    def gather_end(ref, name, r):
        arrived(ref.at[0, pl.ds(0, 3 * PAIR)], (name, "b", r))

    def share(dz):
        return rows16(lax.rem(z + dz, NZ))

    def reduce_step(n, r, t):
        if t == 3 and n == 0:
            arrived(tok.at[0, pl.ds(0, 3 * ROWS)], ("r", n, r, 1))
        elif t > 1:
            arrived(zrcv.at[n, r, 0, 0] if t == 2 else zrcv.at[n, r, t - 2], ("r", n, r, t - 1))
        for way, dev, dev2 in ((0, z_up, z_up2), (1, z_down, z_down2)):
            dz = 5 - t if way == 0 else 3 + t
            near = mine if way == 0 else theirs
            buf, dst = zsnd.at[n, r, t - 1, way], zrcv.at[n, r, t - 1, way]
            if t == 1:
                buf[:, near] = part[n, r, share(dz), near].astype(BF16)
                buf, dst = buf.at[:, near], dst.at[:, near]
                if n == 0:
                    send(buf, dst, ("z", n), ("r", n, r, 1), dev2)
                    buf, dst = zsnd.at[n, r, 1, way], zrcv.at[n, r, 1, way]
                    buf[...] = part[n, r, share(3 if way == 0 else 5)].astype(BF16)
            elif t == 2 or (t == 3 and n == 0):
                there = zrcv[n, r, 1, way].astype(F32) if n == 0 else 0.0
                total = part[n, r, share(dz)] + there
                a, b = total[:, : HID], total[:, HID:]
                extra = zrcv[n, r, 0, way, :, near].astype(F32)
                a, b = (a + extra, b) if way == 0 else (a, b + extra)
                buf[:, mine] = a.astype(BF16)
                buf[:, theirs] = b.astype(BF16)
            else:
                buf[...] = (part[n, r, share(dz)] + zrcv[n, r, t - 2, way].astype(F32)).astype(BF16)
            send(buf, dst, ("z", n), ("r", n, r, t), dev)

    def reduce_end(n, r):
        arrived(zrcv.at[n, r, 3], ("r", n, r, 4))
        return part[n, r, share(0)] + zrcv[n, r, 3, 0].astype(F32) + zrcv[n, r, 3, 1].astype(F32)

    def spread_step(n, r, t):
        ref = grd if n else act
        if t > 1:
            arrived(zrcv.at[n, r, 3], ("s", n, r, t - 1))
        for way, dev in ((0, z_up), (1, z_down)):
            dz = NZ + 1 - t if way == 0 else t - 1
            piece = ref.at[chunk[r], share(dz)]
            near = theirs if way else mine
            if t == 3 and n == 1:
                send(piece.at[:, near], piece.at[:, near], ("z", n), ("s", n, r, t), z_down2 if way else z_up2)
            if t == 4:
                piece = piece.at[:, near]
            send(piece, piece, ("z", n), ("s", n, r, t), dev)
        for dz in (0,) if t == 1 else (NZ + 1 - t, t - 1):
            hand_near(n, r, dz)

    def spread_end(n, r):
        if n == 0:
            arrived(zrcv.at[n, r, 3, 0], ("s", n, r, 4))
        else:
            arrived(tok.at[0, pl.ds(0, 3 * ROWS)], ("s", n, r, 3))
            hand_near(n, r, 3)
            hand_near(n, r, 5)
        hand_near(n, r, 4)

    def hand_near(n, r, dz):
        ref, dst = (grd, grd2) if n else (act, act2)
        send(ref.at[chunk[r], share(dz), theirs], dst.at[chunk[r], share(dz)], "near", ("near", n), sibling)

    def scatter_first(n, r, h):
        for d in (2, 1, 3):
            if h == 0:
                lsnd[n, r, h, d - 1] = part[n, r, pl.ds(d * PAIR, PAIR), cols[h]].astype(BF16)
            else:
                f = lax.rem(chunk[r] + d, 2)
                for i, e in enumerate((0, 2)):
                    lsnd[n, r, h, d - 1, rows16(i)] = part[n, r, rows16((f + e) * 2 + d // 2), cols[h]].astype(BF16)
            send(lsnd.at[n, r, h, d - 1], lrcv.at[n, r, h, d - 1], ("l", n), ("l", n, r, h), along(second[h], d))

    def scatter_second(n, r):
        q = chunk[r]
        for h in halves:
            arrived(lrcv.at[n, r, h], ("l", n, r, h))
            got = [lrcv[n, r, h, d].astype(F32) for d in (0, 1, 2)]
            if h == 0:
                own = part[n, r, pl.ds(0, PAIR), cols[h]]
            else:
                own = jnp.concatenate([part[n, r, rows16((q + e) * 2), cols[h]] for e in (0, 2)], axis=0)
            ssnd[n, r, h] = own + got[0] + got[1] + got[2]
            send(ssnd.at[n, r, h, rows16(1)], srcv.at[n, h, q + 1], ("l", n), ("m", n, h), along(first[h], q + 2))

            @pl.when(q == 1)
            def _():
                send(ssnd.at[n, r, h, rows16(0)], srcv.at[n, h, 0], ("l", n), ("m", n, h), along(first[h], 1), r == 0)

    def scatter_end(n, ref):
        for h in halves:
            arrived(srcv.at[n, h], ("m", n, h))
            total = ssnd[n, parity, h, rows16(0)] + srcv[n, h, 0] + srcv[n, h, 1] + srcv[n, h, 2]
            ref[:, cols[h]] = total.astype(BF16)

    def multiply(n, r):
        if n == 0:
            part[0, r] = mm(tok[chunk[r]], wi[...])
        else:
            part[1, r] = mm(cot[chunk[r]], wot[...])
        reduce_step(n, r, 1)

    def middle(n, r):
        total = reduce_end(n, r)
        if n == 0:
            gelu_out, derivative = activate(total)
            act[chunk[r], share(0)] = gelu_out.astype(BF16)
            slope[r] = derivative
        else:
            grd[chunk[r], share(0)] = (total * slope[r]).astype(BF16)
        spread_step(n, r, 1)

    def finish(n, r):
        spread_end(n, r)
        for h in halves:
            if n == 0:
                part[n, r, :, cols[h]] = mm(act[chunk[r]], wo[:, cols[h]])
            else:
                part[n, r, :, cols[h]] = mm(grd[chunk[r]], wit[:, cols[h]])
            scatter_first(n, r, h)

    def both(ref, first_chunk):
        got = ref[pl.ds(first_chunk, 2)]
        return got.reshape(-1, got.shape[-1])

    def weight_grad(n):
        if n == 0:
            arrived(cot.at[pl.ds(2, 2)], "cot2")
            arrived(act2, ("near", 0))
            total = mm_tn(act[:, :, mine].reshape(MINE, HID), both(cot, 0)) + mm_tn(both(act2, 0), both(cot, 2))
            gwo[...] = total.astype(BF16)
        else:
            arrived(tok.at[pl.ds(2, 2)], "tok2")
            arrived(grd2, ("near", 1))
            total = mm_tn(both(tok, 0), grd[:, :, mine].reshape(MINE, HID)) + mm_tn(both(tok, 2), both(grd2, 0))
            gwi[...] = total.astype(BF16)

    got_tok.wait()
    gather_first(tok, "tok")
    got_wi.wait()
    send(wi.at[:, mine], wi.at[:, theirs], "wi", "wi", sibling)
    got_cot.wait()
    gather_first(cot, "cot")
    got_wo.wait()
    for i in range(3):
        wot[:, pl.ds(i * 256, 256)] = wo[pl.ds(i * 256, 256)].T
    send(wot.at[:, mine], wot.at[:, theirs], "wot", "wot", sibling)
    gather_first_end(tok, "tok")
    gather_second(tok, "tok", 0)
    gather_second(tok, "tok", 1)
    for i in range(3):
        wit[pl.ds(i * 256, 256)] = wi[:, pl.ds(i * 256, 256)].T
    send(wo.at[mine], wo.at[theirs], "wo", "wo", sibling)
    send(wit.at[mine], wit.at[theirs], "wit", "wit", sibling)
    gather_first_end(cot, "cot")
    gather_end(tok, "tok", 0)
    gather_second(cot, "cot", 0)
    arrived(wi.at[:, theirs], "wi")
    multiply(0, 0)
    gather_end(tok, "tok", 1)
    gather_second(cot, "cot", 1)
    multiply(0, 1)
    gather_end(cot, "cot", 0)
    arrived(wot.at[:, theirs], "wot")
    multiply(1, 0)
    reduce_step(0, 0, 3)
    gather_end(cot, "cot", 1)
    multiply(1, 1)
    send(tok.at[pl.ds(0, 2)], tok.at[pl.ds(2, 2)], "near", "tok2", sibling)
    send(cot.at[pl.ds(0, 2)], cot.at[pl.ds(2, 2)], "near", "cot2", sibling)
    reduce_step(0, 1, 3)
    reduce_step(1, 0, 2)
    reduce_step(0, 0, 4)
    reduce_step(1, 1, 2)
    reduce_step(0, 1, 4)
    reduce_step(1, 0, 3)
    middle(0, 0)
    reduce_step(1, 1, 3)
    middle(0, 1)
    reduce_step(1, 0, 4)
    spread_step(0, 0, 2)
    reduce_step(1, 1, 4)
    spread_step(0, 1, 2)
    middle(1, 0)
    spread_step(0, 0, 3)
    middle(1, 1)
    spread_step(0, 1, 3)
    spread_step(1, 0, 2)
    spread_step(0, 0, 4)
    spread_step(1, 1, 2)
    spread_step(0, 1, 4)
    spread_step(1, 0, 3)
    arrived(wo.at[theirs], "wo")
    finish(0, 0)
    spread_step(1, 1, 3)
    finish(0, 1)
    arrived(wit.at[theirs], "wit")
    finish(1, 0)
    finish(1, 1)
    scatter_second(0, 0)
    weight_grad(0)
    scatter_second(1, 0)
    scatter_second(0, 1)
    weight_grad(1)
    scatter_second(1, 1)
    scatter_end(0, out_ref)
    scatter_end(1, gt_ref)
    for s in sent:
        all_sent(s)
    for pool, known in ((ssem, N_SEND), (rsem, N_RECV), (lsem, 4)):
        assert len(names[id(pool)]) <= known, len(names[id(pool)])


def hand_over(*refs):
    srcs, dsts, sems = refs[:4], refs[4:8], refs[8]
    copies = []
    for s, d in zip(srcs, dsts):
        parts = s.shape[0] // 192 or 1
        for p in range(parts):
            rows = pl.ds(p * (s.shape[0] // parts), s.shape[0] // parts)
            copies.append(pltpu.make_async_copy(s.at[rows], d.at[rows], sems.at[len(copies)]))
    for copy in copies:
        copy.start()
    for copy in copies:
        copy.wait()


def per_device(tokens, weight_in, weight_out, cotangent):
    hbm = pl.BlockSpec(memory_space=pltpu.HBM)
    vmem = pl.BlockSpec(memory_space=pltpu.VMEM)
    shape = jax.ShapeDtypeStruct
    shapes = (
        shape((ROWS, FEAT), BF16), shape((ROWS, FEAT), BF16), shape((FEAT, HID), BF16), shape((HID, FEAT), BF16),
    )
    tokens, cotangent = [pltpu.with_memory_space_constraint(a, pltpu.HBM) for a in (tokens, cotangent)]
    results = pl.pallas_call(
        kernel,
        out_shape=shapes,
        in_specs=[hbm] * 4,
        out_specs=(vmem,) * 4,
        scratch_shapes=[
            pltpu.VMEM((FEAT, 2 * HID), BF16),
            pltpu.VMEM((2 * HID, FEAT), BF16),
            pltpu.VMEM((2 * HID, FEAT), BF16),
            pltpu.VMEM((FEAT, 2 * HID), BF16),
            pltpu.VMEM((4, CHUNK, FEAT), BF16),
            pltpu.VMEM((4, CHUNK, FEAT), BF16),
            pltpu.VMEM((2, 2, CHUNK, 2 * HID), F32),
            pltpu.VMEM((2, 2, 4, 2, ROWS, 2 * HID), BF16),
            pltpu.VMEM((2, 2, 4, 2, ROWS, 2 * HID), BF16),
            pltpu.VMEM((2, CHUNK, 2 * HID), BF16),
            pltpu.VMEM((2, CHUNK, 2 * HID), BF16),
            pltpu.VMEM((2, CHUNK, HID), BF16),
            pltpu.VMEM((2, CHUNK, HID), BF16),
            pltpu.VMEM((2, ROWS, 2 * HID), F32),
            pltpu.VMEM((2, 2, 2, 3, PAIR, FH), BF16),
            pltpu.VMEM((2, 2, 2, 3, PAIR, FH), BF16),
            pltpu.VMEM((2, 2, 2, PAIR, FH), F32),
            pltpu.VMEM((2, 2, 3, ROWS, FH), F32),
            pltpu.SemaphoreType.DMA((N_SEND,)),
            pltpu.SemaphoreType.DMA((N_RECV,)),
            pltpu.SemaphoreType.DMA((4,)),
        ],
        compiler_params=pltpu.CompilerParams(
            collective_id=0, has_side_effects=True, vmem_limit_bytes=48 * 2**20
        ),
        cost_estimate=pl.CostEstimate(flops=7 * 10**9, bytes_accessed=10**7, transcendentals=5 * 10**4),
    )(tokens, weight_in, weight_out, cotangent)
    return pl.pallas_call(
        hand_over,
        out_shape=shapes,
        in_specs=[vmem] * 4,
        out_specs=(hbm,) * 4,
        scratch_shapes=[pltpu.SemaphoreType.DMA((14,))],
        compiler_params=pltpu.CompilerParams(vmem_limit_bytes=2**21),
        cost_estimate=pl.CostEstimate(flops=0, bytes_accessed=10**7, transcendentals=0),
    )(*results)


def solution(mesh):
    in_specs = (P("row", "col"), P("col", "row"), P("row", "col"), P("row", "col"))
    out_specs = (P("row", "col"), P("row", "col"), P("col", "row"), P("row", "col"))
    return jax.shard_map(
        per_device, mesh=mesh, in_specs=in_specs, out_specs=out_specs, check_vma=False
    )
```
